32 devices in a mesh: vin: 8 (over z, core), vout: 2 (over x), cell: 2 (over y).
Axes of the slice: x: 2, y: 2, z: 4, core: 2. Of those that a mesh axis runs over, the one named last changes fastest.
Arguments:
- distribution: bfloat16 [8, 13824, 4, 128], P('vout', 'vin', 'cell'), may hold values from -6 to 6
- collision: bfloat16 [13824, 13824], P('vout', 'vin'), may hold values from -1 to 3
- speeds: float32 [3, 13824], P(None, 'vout'), may hold values from 0.05 to 0.3
- directions: int32 [3, 13824], P(None, 'vout'), may hold values from 0 to 1
- cell_flags: int32 [8, 4, 128], P('vin', 'cell'), may hold values 0 or 1
Outputs:
- updated: bfloat16 [8, 13824, 4, 128], P('vin', 'vout', 'cell')
The draws below stay inside these ranges and needn't reach their ends.
Inputs may be any that keep to these rules, and one draw needn't show every extreme that they name: `directions`: 1 means the component is positive, 0 negative. `cell_flags`: 1 marks a solid cell, where nothing is transported.
All inputs are finite; a program needn't handle non-finite values. No bound on the sum of `cell_flags` on one device may be relied on, other than what follows from the above.
Results may differ from the reference program's by a relative error of at most 0.023.
Values may be sent and summed in bfloat16 or wider, within the bound.
A program may use at most 128 MiB of HBM per device.

```python
import jax
import jax.numpy as jnp
from jax import lax

NV = 13824
NX = 128
NZ = 8
NY = 4
N_VIN = 8


def draw_collision(key, part):
    matrix_order = NV
    noise = jnp.clip(jax.random.normal(key, (matrix_order, matrix_order), jnp.float32), -4.0, 4.0)
    diag_value = 1.0
    row_index = lax.broadcasted_iota(jnp.int32, (matrix_order, matrix_order), 0)
    col_index = lax.broadcasted_iota(jnp.int32, (matrix_order, matrix_order), 1)
    identity = jnp.where(row_index == col_index, diag_value, 0.0)
    return (noise * matrix_order ** (-0.5) + identity).astype(jnp.bfloat16)


def touch_ends(values, rng, low, top_value):
    extent = values.shape
    index_at = [jax.random.randint(jax.random.fold_in(rng, axis), (), 0, extent[axis]) for axis in range(len(extent))]
    values = values.at[tuple(index_at)].set(low)
    longest = extent.index(max(extent))
    index_at[longest] = (index_at[longest] + 1) % extent[longest]
    return values.at[tuple(index_at)].set(top_value)


def block_scale(own_key, shape, cuts, low, largest):
    level, own = 1.0, jax.random.fold_in(own_key, 6)
    for position, parts in cuts:
        heights = jnp.exp(jax.random.uniform(jax.random.fold_in(own, position), (parts,), jnp.float32, low / len(cuts), largest / len(cuts)))
        level = level * jnp.repeat(heights, shape[position] // parts).reshape([-1 if axis == position else 1 for axis in range(len(shape))])
    return level


def normal_values(rng, shape, deviation, most, pieces=(), dtype=jnp.bfloat16):
    result = jax.random.normal(rng, shape, jnp.float32) * deviation
    if len(pieces) > 0:
        result = block_scale(rng, shape, pieces, -0.22, 0.18) * result
    return jnp.clip(result, min=-most, max=most).astype(dtype)


def setup_inputs(seed: int = 0) -> dict:
    arg_keys = jax.random.split(jax.random.key(seed), 6)
    distribution = normal_values(arg_keys[0], (NZ, NV, NY, NX), 1.0, 6.0, ((0, 2), (1, 8), (2, 2)))
    collision = draw_collision(jax.random.fold_in(arg_keys[5], 71), 0)
    speeds = jnp.clip(0.05 + 0.25 * jax.random.uniform(arg_keys[2], (3, NV), jnp.float32) ** block_scale(arg_keys[2], (3, NV), ((1, 2),), -0.2, 0.2), 0.05, 0.3)
    directions = touch_ends(jax.random.randint(arg_keys[3], (3, NV), 0, 2), jax.random.fold_in(arg_keys[3], 1), 0, 1).astype(jnp.int32)
    cell_flags = touch_ends((jax.random.randint(arg_keys[4], (NZ, NY, NX), 0, 4) < 1).astype(jnp.int32), jax.random.fold_in(arg_keys[4], 1), 0, 1)
    return dict(distribution=distribution, collision=collision, speeds=speeds, directions=directions, cell_flags=cell_flags)


def transport(padded, speeds, directions, cell_flags):
    field_pad = padded.astype(jnp.float32)
    extended = jnp.pad(field_pad, ((0, 0), (0, 0), (0, 0), (1, 1)))
    center = extended[1:-1, :, 1:-1, 1:-1]
    neighbours = (
        (extended[1:-1, :, 1:-1, :-2], extended[1:-1, :, 1:-1, 2:]),
        (extended[1:-1, :, :-2, 1:-1], extended[1:-1, :, 2:, 1:-1]),
        (extended[:-2, :, 1:-1, 1:-1], extended[2:, :, 1:-1, 1:-1]),
    )
    flux_sum = jnp.zeros_like(center)
    for component in range(3):
        low_side, high_side = neighbours[component]
        positive = (directions[component] == 1)[None, :, None, None]
        upstream = jnp.where(positive, low_side, high_side)
        flux_sum = flux_sum + speeds[component][None, :, None, None] * (center - upstream)
    fluid_mask = (1 - cell_flags).astype(jnp.float32)[:, None, :, :]
    return (center - fluid_mask * flux_sum).astype(jnp.bfloat16)


def reference(distribution, collision, speeds, directions, cell_flags):
    block_size = NV // N_VIN
    dist_wide = distribution.astype(jnp.float32)

    def add_block(index, total):
        offset = jnp.asarray(index, jnp.int32) * block_size
        matrix_cols = lax.dynamic_slice_in_dim(collision, offset, block_size, 1).astype(jnp.float32)
        dist_block = lax.dynamic_slice_in_dim(dist_wide, offset, block_size, 1)
        partial_sum = jnp.einsum("vu,zuyx->zvyx", matrix_cols, dist_block)
        rounded = lax.optimization_barrier(partial_sum.astype(jnp.bfloat16))
        return total + rounded.astype(jnp.float32)

    total = lax.fori_loop(0, N_VIN, add_block, jnp.zeros((NZ, NV, NY, NX), jnp.float32))
    relaxed = total.astype(jnp.bfloat16)
    padded = jnp.pad(relaxed, ((1, 1), (0, 0), (1, 1), (0, 0)))
    return transport(padded, speeds, directions, cell_flags)
```

```python
import jax
import jax.numpy as jnp
from jax import lax
from jax.sharding import PartitionSpec as P

CHUNKS = 4


def from_lower(values, axis):
    ends = lax.axis_size(axis) - 1
    return lax.ppermute(values, axis, [(i, i + 1) for i in range(ends)])


def from_higher(values, axis):
    ends = lax.axis_size(axis) - 1
    return lax.ppermute(values, axis, [(i + 1, i) for i in range(ends)])


def shifted(values, step):
    edge = jnp.zeros_like(values[:, :1])
    if step > 0:
        return jnp.concatenate([edge, values[:, :-1]], axis=1)
    return jnp.concatenate([values[:, 1:], edge], axis=1)


def transport(center, neighbours, speeds, positive, fluid):
    middle = center.astype(jnp.float32)
    flux = jnp.zeros_like(middle)
    for component, (low, high) in enumerate(neighbours):
        upstream = jnp.where(positive[component][:, None], low, high).astype(jnp.float32)
        flux = flux + speeds[component][:, None] * (middle - upstream)
    return (middle - fluid[None, :] * flux).astype(jnp.bfloat16)


def on_device(distribution, collision, speeds, directions, cell_flags):
    rows = distribution.shape[2]
    velocities = collision.shape[0]
    chunk = velocities // CHUNKS
    planes = [
        lax.all_gather(distribution[:, :, row, :], "vout", axis=0, tiled=True)
        for row in range(rows)
    ]
    fluid = (1 - cell_flags[0]).astype(jnp.float32)
    relaxed = [[None] * rows for _ in range(CHUNKS)]
    for row in range(rows):
        for part in range(CHUNKS):
            block = lax.slice_in_dim(collision, part * chunk, (part + 1) * chunk, axis=0)
            partial = jnp.einsum(
                "vu,zux->zvx", block, planes[row], preferred_element_type=jnp.float32
            ).astype(jnp.bfloat16)
            relaxed[part][row] = lax.psum_scatter(
                partial, "vin", scatter_dimension=0, tiled=True
            )[0]
    outs = []
    for part in range(CHUNKS):
        cells = relaxed[part]
        own = slice(part * chunk, (part + 1) * chunk)
        positive = directions[:, own] == 1
        pace = speeds[:, own]
        before = from_lower(cells[-1], "cell")
        after = from_higher(cells[0], "cell")
        column = [before, *cells, after]
        done = []
        for row in range(rows):
            center = cells[row]
            neighbours = (
                (shifted(center, 1), shifted(center, -1)),
                (column[row], column[row + 2]),
                (from_lower(center, "vin"), from_higher(center, "vin")),
            )
            done.append(transport(center, neighbours, pace, positive, fluid[row]))
        outs.append(jnp.stack(done, axis=1))
    return jnp.concatenate(outs, axis=0)[None]


def solution(mesh):
    return jax.shard_map(
        on_device,
        mesh=mesh,
        in_specs=(
            P("vout", "vin", "cell", None),
            P("vout", "vin"),
            P(None, "vout"),
            P(None, "vout"),
            P("vin", "cell", None),
        ),
        out_specs=P("vin", "vout", "cell", None),
        check_vma=False,
    )
```

```python
import jax
import jax.numpy as jnp
from jax import lax
from jax.sharding import PartitionSpec as P

CHUNKS = 4
CORES = 2


def from_lower(values, axis):
    ends = lax.axis_size(axis) - 1
    return lax.ppermute(values, axis, [(i, i + 1) for i in range(ends)])


def from_higher(values, axis):
    ends = lax.axis_size(axis) - 1
    return lax.ppermute(values, axis, [(i + 1, i) for i in range(ends)])


def hop(values, axis, pairs):
    return lax.ppermute(values, axis, pairs)


def core_pairs(axis):
    return [(i, i + 1 - 2 * (i % CORES)) for i in range(lax.axis_size(axis))]


def scatter_line(own, axis):
    chips = lax.axis_size(axis) // CORES
    chip = lax.axis_index(axis) // CORES
    total = lax.dynamic_index_in_dim(own, chip, 0, keepdims=False).astype(jnp.float32)
    up = down = None
    for step in range(chips - 1):
        target = jnp.clip(chips - 1 - step + chip, 0, chips - 1)
        lower = jnp.clip(step - (chips - 1 - chip), 0, chips - 1)
        send_up = lax.dynamic_index_in_dim(own, target, 0, keepdims=False)
        send_down = lax.dynamic_index_in_dim(own, lower, 0, keepdims=False)
        if step:
            send_up = (send_up.astype(jnp.float32) + up.astype(jnp.float32)).astype(own.dtype)
            send_down = (send_down.astype(jnp.float32) + down.astype(jnp.float32)).astype(own.dtype)
        rising, falling = [], []
        for at in range(step + 1):
            mirror = chips - 1 - at
            for core in range(CORES):
                rising.append((at * CORES + core, (at + 1) * CORES + core))
                falling.append((mirror * CORES + core, (mirror - 1) * CORES + core))
        up = hop(send_up, axis, rising)
        down = hop(send_down, axis, falling)
    if up is not None:
        total = total + up.astype(jnp.float32) + down.astype(jnp.float32)
    return total.astype(own.dtype)


def shifted(values, step):
    edge = jnp.zeros_like(values[..., :1])
    if step > 0:
        return jnp.concatenate([edge, values[..., :-1]], axis=-1)
    return jnp.concatenate([values[..., 1:], edge], axis=-1)


def transport(center, neighbours, speeds, positive, fluid):
    middle = center.astype(jnp.float32)
    flux = jnp.zeros_like(middle)
    for component, (low, high) in enumerate(neighbours):
        upstream = jnp.where(positive[component][:, None, None], low, high).astype(jnp.float32)
        flux = flux + speeds[component][:, None, None] * (middle - upstream)
    return (middle - fluid[None] * flux).astype(jnp.bfloat16)


def on_device(distribution, collision, speeds, directions, cell_flags):
    velocities = collision.shape[0]
    chunk = velocities // CHUNKS
    planes = lax.all_gather(distribution, "vout", axis=0, tiled=True)
    planes = planes.reshape((planes.shape[0] // CORES, CORES) + planes.shape[1:])
    core = lax.rem(lax.axis_index("vin"), CORES)
    mine = lax.dynamic_index_in_dim(planes, core, 1, keepdims=False)
    theirs = lax.dynamic_index_in_dim(planes, 1 - core, 1, keepdims=False)
    fluid = (1 - cell_flags[0]).astype(jnp.float32)
    outs = []
    for part in range(CHUNKS):
        own = slice(part * chunk, (part + 1) * chunk)
        block = collision[own]
        spec = "vu,zuyx->zvyx"
        away = jnp.einsum(spec, block, theirs, preferred_element_type=jnp.float32)
        near = jnp.einsum(spec, block, mine, preferred_element_type=jnp.float32)
        got = hop(away.astype(jnp.bfloat16), "vin", core_pairs("vin"))
        both = (near + got.astype(jnp.float32)).astype(jnp.bfloat16)
        cells = scatter_line(both, "vin")
        before = from_lower(cells[:, -1:], "cell")
        after = from_higher(cells[:, :1], "cell")
        neighbours = (
            (shifted(cells, 1), shifted(cells, -1)),
            (
                jnp.concatenate([before, cells[:, :-1]], axis=1),
                jnp.concatenate([cells[:, 1:], after], axis=1),
            ),
            (from_lower(cells, "vin"), from_higher(cells, "vin")),
        )
        outs.append(transport(cells, neighbours, speeds[:, own], directions[:, own] == 1, fluid))
    return jnp.concatenate(outs, axis=0)[None]


def solution(mesh):
    return jax.shard_map(
        on_device,
        mesh=mesh,
        in_specs=(
            P("vout", "vin", "cell", None),
            P("vout", "vin"),
            P(None, "vout"),
            P(None, "vout"),
            P("vin", "cell", None),
        ),
        out_specs=P("vin", "vout", "cell", None),
        check_vma=False,
    )
```

```python
import jax
import jax.numpy as jnp
from jax import lax
from jax.sharding import PartitionSpec as P

CHUNKS = 3
CORES = 2


def from_lower(values, axis):
    ends = lax.axis_size(axis) - 1
    return lax.ppermute(values, axis, [(i, i + 1) for i in range(ends)])


def from_higher(values, axis):
    ends = lax.axis_size(axis) - 1
    return lax.ppermute(values, axis, [(i + 1, i) for i in range(ends)])


def hop(values, axis, pairs):
    return lax.ppermute(values, axis, pairs)


def core_pairs(axis):
    return [(i, i + 1 - 2 * (i % CORES)) for i in range(lax.axis_size(axis))]


def scatter_line(own, axis):
    chips = lax.axis_size(axis) // CORES
    chip = lax.axis_index(axis) // CORES
    total = lax.dynamic_index_in_dim(own, chip, 0, keepdims=False).astype(jnp.float32)
    up = down = None
    for step in range(chips - 1):
        target = jnp.clip(chips - 1 - step + chip, 0, chips - 1)
        lower = jnp.clip(step - (chips - 1 - chip), 0, chips - 1)
        send_up = lax.dynamic_index_in_dim(own, target, 0, keepdims=False)
        send_down = lax.dynamic_index_in_dim(own, lower, 0, keepdims=False)
        if step:
            send_up = (send_up.astype(jnp.float32) + up.astype(jnp.float32)).astype(own.dtype)
            send_down = (send_down.astype(jnp.float32) + down.astype(jnp.float32)).astype(own.dtype)
        rising, falling = [], []
        for at in range(step + 1):
            mirror = chips - 1 - at
            for core in range(CORES):
                rising.append((at * CORES + core, (at + 1) * CORES + core))
                falling.append((mirror * CORES + core, (mirror - 1) * CORES + core))
        up = hop(send_up, axis, rising)
        down = hop(send_down, axis, falling)
    if up is not None:
        total = total + up.astype(jnp.float32) + down.astype(jnp.float32)
    return total.astype(own.dtype)


def shifted(values, step):
    edge = jnp.zeros_like(values[..., :1])
    if step > 0:
        return jnp.concatenate([edge, values[..., :-1]], axis=-1)
    return jnp.concatenate([values[..., 1:], edge], axis=-1)


def transport(center, neighbours, speeds, positive, fluid):
    middle = center.astype(jnp.float32)
    flux = jnp.zeros_like(middle)
    for component, (low, high) in enumerate(neighbours):
        upstream = jnp.where(positive[component][:, None, None], low, high).astype(jnp.float32)
        flux = flux + speeds[component][:, None, None] * (middle - upstream)
    return (middle - fluid[None] * flux).astype(jnp.bfloat16)


def on_device(distribution, collision, speeds, directions, cell_flags):
    velocities = collision.shape[0]
    chunk = velocities // CHUNKS
    planes = lax.all_gather(distribution, "vout", axis=0, tiled=True)
    planes = planes.reshape((planes.shape[0] // CORES, CORES) + planes.shape[1:])
    core = lax.rem(lax.axis_index("vin"), CORES)
    mine = lax.dynamic_index_in_dim(planes, core, 1, keepdims=False)
    theirs = lax.dynamic_index_in_dim(planes, 1 - core, 1, keepdims=False)
    fluid = (1 - cell_flags[0]).astype(jnp.float32)
    outs = []
    for part in range(CHUNKS):
        own = slice(part * chunk, (part + 1) * chunk)
        block = collision[own]
        spec = "vu,zuyx->zvyx"
        away = jnp.einsum(spec, block, theirs, preferred_element_type=jnp.float32)
        near = jnp.einsum(spec, block, mine, preferred_element_type=jnp.float32)
        got = hop(away.astype(jnp.bfloat16), "vin", core_pairs("vin"))
        both = (near + got.astype(jnp.float32)).astype(jnp.bfloat16)
        cells = scatter_line(both, "vin")
        before = from_lower(cells[:, -1:], "cell")
        after = from_higher(cells[:, :1], "cell")
        neighbours = (
            (shifted(cells, 1), shifted(cells, -1)),
            (
                jnp.concatenate([before, cells[:, :-1]], axis=1),
                jnp.concatenate([cells[:, 1:], after], axis=1),
            ),
            (from_lower(cells, "vin"), from_higher(cells, "vin")),
        )
        outs.append(transport(cells, neighbours, speeds[:, own], directions[:, own] == 1, fluid))
    return jnp.concatenate(outs, axis=0)[None]


def solution(mesh):
    return jax.shard_map(
        on_device,
        mesh=mesh,
        in_specs=(
            P("vout", "vin", "cell", None),
            P("vout", "vin"),
            P(None, "vout"),
            P(None, "vout"),
            P("vin", "cell", None),
        ),
        out_specs=P("vin", "vout", "cell", None),
        check_vma=False,
    )
```
